32 devices in a mesh: row: 8 (over z, core), col: 4 (over y, x).
Axes of the slice: x: 2, y: 2, z: 4, core: 2. Of those that a mesh axis runs over, the one named last changes fastest.
Arguments:
- covariance: float32 [1, 8192, 8192], P(None, 'row', 'col'), may hold values from -120 to 120, as said below
- latitude_offset: int32 [1, 1, 8192], replicated, may hold values from -2 to 2
- longitude_offset: int32 [1, 1, 8192], replicated, may hold values from -3 to 3
- upwind: int32 [1, 1, 8192], replicated, may hold values from 0 to 3
- courant: float32 [1, 1, 8192], replicated, may hold values from 0.05 to 0.45
- longitude_diffusion: float32 [1, 8192], replicated, may hold values from 0.01 to 0.08
- latitude_diffusion: float32 [1, 8192], replicated, may hold values from 0.01 to 0.08
Outputs:
- forecast_cov: float32 [1, 8192, 8192], P(None, 'row', 'col')
The draws below stay inside these ranges and needn't reach their ends.
Inputs may be any that keep to these rules, and one draw needn't show every extreme that they name: `covariance`: each level's matrix is symmetric up to rounding.
All inputs are finite; a program needn't handle non-finite values.
Results may differ from the reference program's by a relative error of at most 0.0003.
Values sent between devices are 32-bit elements; how exact they have to be, the bound alone decides.
A program may use at most 128 MiB of HBM per device.

```python
import jax
import jax.numpy as jnp
from jax import lax

NLAT = 64
NLON = 128
NV = 8192
STEPS = 1
LEV = 1


def draw_covariance(key, part):
    base_key = jax.random.fold_in(key, 7)
    key_noise, key_diag = jax.random.split(base_key, 2)
    noise_part = 3.0 * jax.random.truncated_normal(key_noise, -4.0, 4.0, (LEV, NV, NV), jnp.float32)
    symmetric = (noise_part + jnp.swapaxes(noise_part, 1, 2)) * 0.7071
    diagonal_part = jax.random.uniform(key_diag, (LEV, NV), jnp.float32, 4.0, 12.0)
    matrix = symmetric + jnp.eye(NV, dtype=jnp.float32)[None] * diagonal_part[:, :, None]
    return matrix


def touch_ends(entries, own_key, low, top_value):
    shape = entries.shape
    spot = [jax.random.randint(jax.random.fold_in(own_key, axis), (), 0, shape[axis]) for axis in range(len(shape))]
    entries = entries.at[tuple(spot)].set(low)
    longest = shape.index(max(shape))
    spot[longest] = (spot[longest] + 1) % shape[longest]
    return entries.at[tuple(spot)].set(top_value)


def setup_inputs(seed: int = 0) -> dict:
    seeds = jax.random.split(jax.random.key(seed), 8)
    return {
        "covariance": draw_covariance(jax.random.fold_in(seeds[7], 71), 0),
        "latitude_offset": touch_ends(jax.random.randint(seeds[1], (LEV, STEPS, NV), -2, 3), jax.random.fold_in(seeds[1], 1), -2, 2).astype(jnp.int32),
        "longitude_offset": touch_ends(jax.random.randint(seeds[2], (LEV, STEPS, NV), -3, 4), jax.random.fold_in(seeds[2], 1), -3, 3).astype(jnp.int32),
        "upwind": touch_ends(jax.random.randint(seeds[3], (LEV, STEPS, NV), 0, 4), jax.random.fold_in(seeds[3], 1), 0, 3).astype(jnp.int32),
        "courant": jnp.clip(jax.random.uniform(seeds[4], (LEV, STEPS, NV), jnp.float32, 0.05, 0.45), 0.05, 0.45),
        "longitude_diffusion": jnp.clip(jax.random.uniform(seeds[5], (LEV, NV), jnp.float32, 0.01, 0.08), 0.01, 0.08),
        "latitude_diffusion": jnp.clip(jax.random.uniform(seeds[6], (LEV, NV), jnp.float32, 0.01, 0.08), 0.01, 0.08),
    }


def predicted_covariance(field_stack, latitude_offset, longitude_offset, upwind, courant, longitude_diffusion, latitude_diffusion):
    cell_index = jnp.arange(NLAT * NLON, dtype=jnp.int32)
    lat_cell = cell_index // NLON
    lon_cell = cell_index % NLON
    lon_coeff = longitude_diffusion.reshape(NLAT, NLON)
    lat_coeff = latitude_diffusion.reshape(NLAT, NLON)
    cells_total = NLAT * NLON
    for substep in range(STEPS):
        lat_depart = jnp.clip(lat_cell + latitude_offset[substep], 0, NLAT - 1)
        lon_depart = (lon_cell + longitude_offset[substep]) % NLON
        up_code = upwind[substep]
        lat_near = jnp.clip(lat_depart + (up_code == 2).astype(jnp.int32) - (up_code == 3).astype(jnp.int32), 0, NLAT - 1)
        lon_near = (lon_depart + (up_code == 0).astype(jnp.int32) - (up_code == 1).astype(jnp.int32)) % NLON
        depart = (lat_depart * NLON + lon_depart).astype(jnp.int32)
        near = (lat_near * NLON + lon_near).astype(jnp.int32)
        both_index = jnp.concatenate([depart, near]).astype(jnp.int32)
        picked = jnp.take(field_stack, both_index, axis=1)
        weight = courant[substep]
        shifted = (1.0 - weight) * picked[:, :cells_total] + weight * picked[:, cells_total:]
        grid_view = shifted.reshape(shifted.shape[0], NLAT, NLON)
        east_side = jnp.roll(grid_view, -1, axis=2)
        west_side = jnp.roll(grid_view, 1, axis=2)
        north_side = jnp.concatenate([grid_view[:, 1:], grid_view[:, -1:]], axis=1)
        south_side = jnp.concatenate([grid_view[:, :1], grid_view[:, :-1]], axis=1)
        grid_view = grid_view + lon_coeff * (east_side + west_side - 2.0 * grid_view) + lat_coeff * (north_side + south_side - 2.0 * grid_view)
        field_stack = grid_view.reshape(shifted.shape[0], NLAT * NLON)
    return field_stack


def apply_rows(matrix, latitude_offset, longitude_offset, upwind, courant, longitude_diffusion, latitude_diffusion):
    block_rows = min(512, NV)
    block_groups = matrix.reshape(NV // block_rows, block_rows, NV)
    finished_work = lax.map(lambda block_portion: predicted_covariance(block_portion, latitude_offset, longitude_offset, upwind, courant, longitude_diffusion, latitude_diffusion), block_groups)
    return finished_work.reshape(NV, NV)


def reference(covariance, latitude_offset, longitude_offset, upwind, courant, longitude_diffusion, latitude_diffusion):
    def one_level(operands):
        matrix, lat_one, lon_one, up_one, cour_one, flon_one, flat_one = operands
        half_done = apply_rows(matrix, lat_one, lon_one, up_one, cour_one, flon_one, flat_one)
        full_done = apply_rows(half_done.T, lat_one, lon_one, up_one, cour_one, flon_one, flat_one)
        return full_done.T

    return lax.map(one_level, (covariance, latitude_offset, longitude_offset, upwind, courant, longitude_diffusion, latitude_diffusion))
```

```python
import functools

import jax
import jax.numpy as jnp
from jax import lax
from jax.experimental import pallas as pl
from jax.experimental.pallas import tpu as pltpu
from jax.sharding import PartitionSpec as P

NLAT = 64
NLON = 128
TAPS = 10
REACH = 4
HALO = REACH * NLON
PAIR = 2 * NLON
BAND = PAIR + 2 * HALO
EDGE = HALO
MIB = 1024 * 1024


def operator_taps(latitude_offset, longitude_offset, upwind, courant, longitude_diffusion, latitude_diffusion):
    cell = jnp.arange(NLAT * NLON, dtype=jnp.int32)
    lat_depart = jnp.clip(cell // NLON + latitude_offset, 0, NLAT - 1)
    lon_depart = (cell % NLON + longitude_offset) % NLON
    lat_near = jnp.clip(
        lat_depart + (upwind == 2).astype(jnp.int32) - (upwind == 3).astype(jnp.int32), 0, NLAT - 1
    )
    lon_near = (
        lon_depart + (upwind == 0).astype(jnp.int32) - (upwind == 1).astype(jnp.int32)
    ) % NLON
    depart = (lat_depart * NLON + lon_depart).reshape(NLAT, NLON)
    near = (lat_near * NLON + lon_near).reshape(NLAT, NLON)
    weight = courant.reshape(NLAT, NLON)
    lon_c = longitude_diffusion.reshape(NLAT, NLON)
    lat_c = latitude_diffusion.reshape(NLAT, NLON)

    def five(grid):
        return [
            grid,
            jnp.roll(grid, -1, axis=1),
            jnp.roll(grid, 1, axis=1),
            jnp.concatenate([grid[1:], grid[-1:]], axis=0),
            jnp.concatenate([grid[:1], grid[:-1]], axis=0),
        ]

    coeffs = [1.0 - 2.0 * lon_c - 2.0 * lat_c, lon_c, lon_c, lat_c, lat_c]
    far = [f * (1.0 - w) for f, w in zip(coeffs, five(weight))]
    close = [f * w for f, w in zip(coeffs, five(weight))]
    base = ((cell // PAIR) * PAIR - HALO).reshape(NLAT, NLON)
    source = jnp.stack([s - base for s in five(depart) + five(near)]).reshape(TAPS, -1)
    return source, jnp.stack(far + close).reshape(TAPS, -1)


def band_kernel(source_ref, weight_ref, high_ref, low_ref, *, turned):
    lon = lax.broadcasted_iota(jnp.int32, (NLON, PAIR), 0)
    for row in range(BAND // NLON):
        here = lon + row * NLON
        total = jnp.zeros((NLON, PAIR), jnp.float32)
        for tap in range(TAPS):
            total += jnp.where(here == source_ref[tap : tap + 1, :], weight_ref[tap : tap + 1, :], 0.0)
        if turned:
            total = total.T
        high = total.astype(jnp.bfloat16)
        low = (total - high.astype(jnp.float32)).astype(jnp.bfloat16)
        where = pl.ds(row * NLON, NLON)
        if turned:
            high_ref[0, :, where] = high
            low_ref[0, :, where] = low
        else:
            high_ref[0, where, :] = high
            low_ref[0, where, :] = low


def build_bands(source, weight, turned):
    pairs = source.shape[1] // PAIR
    shape = (PAIR, BAND) if turned else (BAND, PAIR)
    out = jax.ShapeDtypeStruct((pairs,) + shape, jnp.bfloat16)
    taps = pl.BlockSpec((TAPS, PAIR), lambda p: (0, p))
    block = pl.BlockSpec((1,) + shape, lambda p: (p, 0, 0))
    return pl.pallas_call(
        functools.partial(band_kernel, turned=turned),
        grid=(pairs,),
        in_specs=[taps, taps],
        out_specs=[block, block],
        out_shape=[out, out],
        compiler_params=pltpu.CompilerParams(vmem_limit_bytes=32 * MIB),
        cost_estimate=pl.CostEstimate(
            flops=pairs * BAND * PAIR * 3 * TAPS * 16, bytes_accessed=pairs * BAND * PAIR * 4, transcendentals=0
        ),
    )(source, weight)


def halves(x):
    high = x.astype(jnp.bfloat16)
    return high, (x - high.astype(jnp.float32)).astype(jnp.bfloat16)


def dot(a, b):
    return jnp.dot(a, b, preferred_element_type=jnp.float32)


def right_kernel(*refs, parts, pairs):
    x_refs, (high_ref, low_ref, out_ref) = refs[:parts], refs[parts:]
    split = [halves(r[...]) for r in x_refs]
    high = jnp.concatenate([s[0] for s in split], axis=1) if parts > 1 else split[0][0]
    low = jnp.concatenate([s[1] for s in split], axis=1) if parts > 1 else split[0][1]
    for p in range(pairs):
        xh = high[:, p * PAIR : p * PAIR + BAND]
        xl = low[:, p * PAIR : p * PAIR + BAND]
        out_ref[:, p * PAIR : (p + 1) * PAIR] = (
            dot(xh, low_ref[p]) + dot(xl, high_ref[p]) + dot(xh, high_ref[p])
        )


def apply_right(parts, high, low, first, pairs, tile=256):
    rows = parts[0][0].shape[0]
    tile = min(tile, rows)
    specs = [pl.BlockSpec((tile, w), lambda i, k=start // w: (i, k)) for _, start, w in parts]
    high, low = high[first : first + pairs], low[first : first + pairs]
    bands = pl.BlockSpec((pairs, BAND, PAIR), lambda i: (0, 0, 0))
    width = pairs * PAIR
    return pl.pallas_call(
        functools.partial(right_kernel, parts=len(parts), pairs=pairs),
        grid=(rows // tile,),
        in_specs=specs + [bands, bands],
        out_specs=pl.BlockSpec((tile, width), lambda i: (i, 0)),
        out_shape=jax.ShapeDtypeStruct((rows, width), jnp.float32),
        compiler_params=pltpu.CompilerParams(vmem_limit_bytes=48 * MIB),
        cost_estimate=pl.CostEstimate(
            flops=6 * rows * BAND * width, bytes_accessed=rows * width * 12, transcendentals=0
        ),
    )(*[p[0] for p in parts], high, low)


def left_kernel(up_ref, own_ref, down_ref, high_ref, low_ref, out_ref, *, pairs):
    split = [halves(r[...]) for r in (up_ref, own_ref, down_ref)]
    high = jnp.concatenate([s[0] for s in split], axis=0)
    low = jnp.concatenate([s[1] for s in split], axis=0)
    for q in range(pairs):
        xh = high[q * PAIR : q * PAIR + BAND]
        xl = low[q * PAIR : q * PAIR + BAND]
        out_ref[q * PAIR : (q + 1) * PAIR, :] = (
            dot(low_ref[q], xh) + dot(high_ref[q], xl) + dot(high_ref[q], xh)
        )


def apply_left(up, own, down, high, low, tile=256):
    rows, width = own.shape
    tile = min(tile, width)
    pairs = rows // PAIR
    column = lambda i: (0, i)
    bands = pl.BlockSpec((pairs, PAIR, BAND), lambda i: (0, 0, 0))
    return pl.pallas_call(
        functools.partial(left_kernel, pairs=pairs),
        grid=(width // tile,),
        in_specs=[
            pl.BlockSpec((HALO, tile), column),
            pl.BlockSpec((rows, tile), column),
            pl.BlockSpec((HALO, tile), column),
            bands,
            bands,
        ],
        out_specs=pl.BlockSpec((rows, tile), column),
        out_shape=jax.ShapeDtypeStruct((rows, width), jnp.float32),
        compiler_params=pltpu.CompilerParams(vmem_limit_bytes=48 * MIB),
        cost_estimate=pl.CostEstimate(
            flops=6 * rows * BAND * width, bytes_accessed=rows * width * 12, transcendentals=0
        ),
    )(up, own, down, high, low)


def shift(x, axis, step):
    count = lax.axis_size(axis)
    return lax.ppermute(x, axis, [(i, i + step) for i in range(count) if 0 <= i + step < count])


def row_halo(half):
    return shift(half[-HALO:], "row", 1), shift(half[:HALO], "row", -1)


def body(covariance, *fields):
    levels, block_rows, block_cols = covariance.shape

    def one_level(field, *level):
        lat, lon, up, cour, flon, flat = level
        west = shift(field[:, block_cols - HALO :], "col", 1)
        east = shift(field[:, :HALO], "col", -1)
        source, weight = operator_taps(lat[0], lon[0], up[0], cour[0], flon, flat)
        col0 = lax.axis_index("col") * block_cols
        row0 = lax.axis_index("row") * block_rows
        cut = lambda a, at, size: lax.dynamic_slice(a, (0, at), (TAPS, size))
        col_high, col_low = build_bands(cut(source, col0, block_cols), cut(weight, col0, block_cols), False)
        row_high, row_low = build_bands(cut(source, row0, block_rows), cut(weight, row0, block_rows), True)
        pairs = block_cols // PAIR
        edge_pairs = EDGE // PAIR
        inner_pairs = pairs - 2 * edge_pairs
        reach = BAND - PAIR
        done = []
        if inner_pairs:
            inner = apply_right([(field, 0, block_cols)], col_high, col_low, edge_pairs, inner_pairs)
            up_in, down_in = row_halo(inner)
            done.append(apply_left(up_in, inner, down_in, row_high, row_low))
        left = apply_right([(west, 0, HALO), (field, 0, reach)], col_high, col_low, 0, edge_pairs)
        right = apply_right(
            [(field, block_cols - reach, reach), (east, 0, HALO)], col_high, col_low, pairs - edge_pairs, edge_pairs
        )
        up_l, down_l = row_halo(left)
        up_r, down_r = row_halo(right)
        out_l = apply_left(up_l, left, down_l, row_high, row_low)
        out_r = apply_left(up_r, right, down_r, row_high, row_low)
        return jnp.concatenate([out_l] + done + [out_r], axis=1)

    return jnp.stack([one_level(covariance[k], *[f[k] for f in fields]) for k in range(levels)])


def solution(mesh):
    in_specs = (P(None, "row", "col"), P(), P(), P(), P(), P(), P())
    out_specs = P(None, "row", "col")
    return jax.shard_map(body, mesh=mesh, in_specs=in_specs, out_specs=out_specs, check_vma=False)
```

```python
import functools

import jax
import jax.numpy as jnp
from jax import lax
from jax.experimental import pallas as pl
from jax.experimental.pallas import tpu as pltpu
from jax.sharding import PartitionSpec as P

NLAT = 64
NLON = 128
TAPS = 10
REACH = 4
HALO = REACH * NLON
PAIR = 2 * NLON
BAND = PAIR + 2 * HALO
EDGE = HALO
MIB = 1024 * 1024


def operator_taps(latitude_offset, longitude_offset, upwind, courant, longitude_diffusion, latitude_diffusion):
    cell = jnp.arange(NLAT * NLON, dtype=jnp.int32)
    lat_depart = jnp.clip(cell // NLON + latitude_offset, 0, NLAT - 1)
    lon_depart = (cell % NLON + longitude_offset) % NLON
    lat_near = jnp.clip(
        lat_depart + (upwind == 2).astype(jnp.int32) - (upwind == 3).astype(jnp.int32), 0, NLAT - 1
    )
    lon_near = (
        lon_depart + (upwind == 0).astype(jnp.int32) - (upwind == 1).astype(jnp.int32)
    ) % NLON
    depart = (lat_depart * NLON + lon_depart).reshape(NLAT, NLON)
    near = (lat_near * NLON + lon_near).reshape(NLAT, NLON)
    weight = courant.reshape(NLAT, NLON)
    lon_c = longitude_diffusion.reshape(NLAT, NLON)
    lat_c = latitude_diffusion.reshape(NLAT, NLON)

    def five(grid):
        return [
            grid,
            jnp.roll(grid, -1, axis=1),
            jnp.roll(grid, 1, axis=1),
            jnp.concatenate([grid[1:], grid[-1:]], axis=0),
            jnp.concatenate([grid[:1], grid[:-1]], axis=0),
        ]

    coeffs = [1.0 - 2.0 * lon_c - 2.0 * lat_c, lon_c, lon_c, lat_c, lat_c]
    far = [f * (1.0 - w) for f, w in zip(coeffs, five(weight))]
    close = [f * w for f, w in zip(coeffs, five(weight))]
    base = ((cell // PAIR) * PAIR - HALO).reshape(NLAT, NLON)
    source = jnp.stack([s - base for s in five(depart) + five(near)]).reshape(TAPS, -1)
    return source, jnp.stack(far + close).reshape(TAPS, -1)


def band_kernel(source_ref, weight_ref, high_ref, low_ref, *, turned):
    lon = lax.broadcasted_iota(jnp.int32, (NLON, PAIR), 0)
    for row in range(BAND // NLON):
        here = lon + row * NLON
        total = jnp.zeros((NLON, PAIR), jnp.float32)
        for tap in range(TAPS):
            total += jnp.where(here == source_ref[tap : tap + 1, :], weight_ref[tap : tap + 1, :], 0.0)
        if turned:
            total = total.T
        high = total.astype(jnp.bfloat16)
        low = (total - high.astype(jnp.float32)).astype(jnp.bfloat16)
        where = pl.ds(row * NLON, NLON)
        if turned:
            high_ref[0, :, where] = high
            low_ref[0, :, where] = low
        else:
            high_ref[0, where, :] = high
            low_ref[0, where, :] = low


def build_bands(source, weight, turned):
    pairs = source.shape[1] // PAIR
    shape = (PAIR, BAND) if turned else (BAND, PAIR)
    out = jax.ShapeDtypeStruct((pairs,) + shape, jnp.bfloat16)
    taps = pl.BlockSpec((TAPS, PAIR), lambda p: (0, p))
    block = pl.BlockSpec((1,) + shape, lambda p: (p, 0, 0))
    return pl.pallas_call(
        functools.partial(band_kernel, turned=turned),
        grid=(pairs,),
        in_specs=[taps, taps],
        out_specs=[block, block],
        out_shape=[out, out],
        compiler_params=pltpu.CompilerParams(vmem_limit_bytes=32 * MIB),
        cost_estimate=pl.CostEstimate(
            flops=pairs * BAND * PAIR * 3 * TAPS * 16, bytes_accessed=pairs * BAND * PAIR * 4, transcendentals=0
        ),
    )(source, weight)


def halves(x):
    high = x.astype(jnp.bfloat16)
    return high, (x - high.astype(jnp.float32)).astype(jnp.bfloat16)


def dot(a, b):
    return jnp.dot(a, b, preferred_element_type=jnp.float32)


def right_kernel(*refs, parts, pairs):
    x_refs, (high_ref, low_ref, out_ref) = refs[:parts], refs[parts:]
    split = [halves(r[...]) for r in x_refs]
    high = jnp.concatenate([s[0] for s in split], axis=1) if parts > 1 else split[0][0]
    low = jnp.concatenate([s[1] for s in split], axis=1) if parts > 1 else split[0][1]
    for p in range(pairs):
        xh = high[:, p * PAIR : p * PAIR + BAND]
        xl = low[:, p * PAIR : p * PAIR + BAND]
        out_ref[:, p * PAIR : (p + 1) * PAIR] = (
            dot(xh, low_ref[p]) + dot(xl, high_ref[p]) + dot(xh, high_ref[p])
        )


def apply_right(parts, high, low, first, pairs, tile=256):
    rows = parts[0][0].shape[0]
    tile = min(tile, rows)
    specs = [pl.BlockSpec((tile, w), lambda i, k=start // w: (i, k)) for _, start, w in parts]
    high, low = high[first : first + pairs], low[first : first + pairs]
    bands = pl.BlockSpec((pairs, BAND, PAIR), lambda i: (0, 0, 0))
    width = pairs * PAIR
    return pl.pallas_call(
        functools.partial(right_kernel, parts=len(parts), pairs=pairs),
        grid=(rows // tile,),
        in_specs=specs + [bands, bands],
        out_specs=pl.BlockSpec((tile, width), lambda i: (i, 0)),
        out_shape=jax.ShapeDtypeStruct((rows, width), jnp.float32),
        compiler_params=pltpu.CompilerParams(vmem_limit_bytes=48 * MIB),
        cost_estimate=pl.CostEstimate(
            flops=6 * rows * BAND * width, bytes_accessed=rows * width * 12, transcendentals=0
        ),
    )(*[p[0] for p in parts], high, low)


def left_kernel(up_ref, own_ref, down_ref, high_ref, low_ref, *rest, pairs):
    out_ref = rest[-1]
    split = [halves(r[...]) for r in (up_ref, own_ref, down_ref)]
    high = jnp.concatenate([s[0] for s in split], axis=0)
    low = jnp.concatenate([s[1] for s in split], axis=0)
    for q in range(pairs):
        xh = high[q * PAIR : q * PAIR + BAND]
        xl = low[q * PAIR : q * PAIR + BAND]
        out_ref[q * PAIR : (q + 1) * PAIR, :] = (
            dot(low_ref[q], xh) + dot(high_ref[q], xl) + dot(high_ref[q], xh)
        )


def apply_left(up, own, down, high, low, start, total, before, tile=256):
    kept = [] if before is None else [before]
    rows, width = own.shape
    tile = min(tile, width)
    pairs = rows // PAIR
    column = lambda i: (0, i)
    bands = pl.BlockSpec((pairs, PAIR, BAND), lambda i: (0, 0, 0))
    return pl.pallas_call(
        functools.partial(left_kernel, pairs=pairs),
        grid=(width // tile,),
        in_specs=[
            pl.BlockSpec((HALO, tile), column),
            pl.BlockSpec((rows, tile), column),
            pl.BlockSpec((HALO, tile), column),
            bands,
            bands,
        ]
        + [pl.BlockSpec(memory_space=pl.ANY)] * len(kept),
        out_specs=pl.BlockSpec((rows, tile), lambda i: (0, start // tile + i)),
        out_shape=jax.ShapeDtypeStruct((rows, total), jnp.float32),
        input_output_aliases={5: 0} if kept else {},
        compiler_params=pltpu.CompilerParams(vmem_limit_bytes=48 * MIB),
        cost_estimate=pl.CostEstimate(
            flops=6 * rows * BAND * width, bytes_accessed=rows * width * 12, transcendentals=0
        ),
    )(up, own, down, high, low, *kept)


def shift(x, axis, step):
    count = lax.axis_size(axis)
    return lax.ppermute(x, axis, [(i, i + step) for i in range(count) if 0 <= i + step < count])


def row_halo(half):
    return shift(half[-HALO:], "row", 1), shift(half[:HALO], "row", -1)


def body(covariance, *fields):
    levels, block_rows, block_cols = covariance.shape

    def one_level(field, *level):
        lat, lon, up, cour, flon, flat = level
        west = shift(field[:, block_cols - HALO :], "col", 1)
        east = shift(field[:, :HALO], "col", -1)
        source, weight = operator_taps(lat[0], lon[0], up[0], cour[0], flon, flat)
        col0 = lax.axis_index("col") * block_cols
        row0 = lax.axis_index("row") * block_rows
        cut = lambda a, at, size: lax.dynamic_slice(a, (0, at), (TAPS, size))
        col_high, col_low = build_bands(cut(source, col0, block_cols), cut(weight, col0, block_cols), False)
        row_high, row_low = build_bands(cut(source, row0, block_rows), cut(weight, row0, block_rows), True)
        pairs = block_cols // PAIR
        edge_pairs = EDGE // PAIR
        inner_pairs = pairs - 2 * edge_pairs
        reach = BAND - PAIR
        result = None
        if inner_pairs:
            inner = apply_right([(field, 0, block_cols)], col_high, col_low, edge_pairs, inner_pairs)
            up_in, down_in = row_halo(inner)
            result = apply_left(up_in, inner, down_in, row_high, row_low, EDGE, block_cols, None)
        left = apply_right([(west, 0, HALO), (field, 0, reach)], col_high, col_low, 0, edge_pairs)
        right = apply_right(
            [(field, block_cols - reach, reach), (east, 0, HALO)], col_high, col_low, pairs - edge_pairs, edge_pairs
        )
        up_l, down_l = row_halo(left)
        up_r, down_r = row_halo(right)
        result = apply_left(up_l, left, down_l, row_high, row_low, 0, block_cols, result)
        return apply_left(up_r, right, down_r, row_high, row_low, block_cols - EDGE, block_cols, result)

    return jnp.stack([one_level(covariance[k], *[f[k] for f in fields]) for k in range(levels)])


def solution(mesh):
    in_specs = (P(None, "row", "col"), P(), P(), P(), P(), P(), P())
    out_specs = P(None, "row", "col")
    return jax.shard_map(body, mesh=mesh, in_specs=in_specs, out_specs=out_specs, check_vma=False)
```
